512 devices in a mesh: dp: 32 (over y, x, core), mem: 16 (over z).
Axes of the slice: x: 4, y: 4, z: 16, core: 2. Of those that a mesh axis runs over, the one named last changes fastest.
Arguments:
- queries: bfloat16 [32, 2048, 2048], P('dp', 'mem'), may hold values from -6 to 6
- seg_keys: bfloat16 [32, 2048, 2048], P('dp', 'mem'), may hold values from -6 to 6
- seg_values: bfloat16 [32, 2048, 2048], P('dp', 'mem'), may hold values from -6 to 6
- mem_keys: bfloat16 [32, 2, 16, 128, 2048], P('dp', None, 'mem'), may hold values from -6 to 6
- mem_values: bfloat16 [32, 2, 16, 128, 2048], P('dp', None, 'mem'), may hold values from -6 to 6
- block_ids: int32 [32, 16, 16, 16], P('dp', None, 'mem'), may hold values from 0 to 31, as said below
- pointer: int32 [32], P('dp'), may hold values from 0 to 16, as said below
- gate_bias: float32 [16], P('mem'), may hold values from -2 to 2
- out_weight: bfloat16 [2048, 2048], P('dp'), may hold values from -0.125 to 0.125
Outputs:
- layer_out: bfloat16 [32, 2048, 2048], P('dp', 'mem')
The draws below stay inside these ranges and needn't reach their ends.
Inputs may be any that keep to these rules, and one draw needn't show every extreme that they name: `pointer`: a multiple of 16. `block_ids`: for each query block and head 16 distinct slots; query block i never names slot pointer + j with j >= i.
All inputs are finite; a program needn't handle non-finite values.
Results may differ from the reference program's by a relative error of at most 0.0056.
Values may be sent and summed in bfloat16 or wider, within the bound.
A program may use at most 64 MiB of HBM per device.

```python
import math
import jax
import jax.numpy as jnp
from jax import lax

D = 2048
H = 16
HD = 128
BLK = 128
MB_DEV = 2
ROWS = 32
SEG = 2048
SEG_BLOCKS = 16
MEM_BLOCKS = 32
TOPK = 16
N_MEM = 16


def pointer_slots(key):
    picked = jax.random.randint(jax.random.fold_in(key, 7), (ROWS,), 0, MEM_BLOCKS // SEG_BLOCKS)
    return (picked * SEG_BLOCKS).astype(jnp.int32)


def draw_queries(key, part):
    key = jax.random.fold_in(key, 1)
    field = jax.random.truncated_normal(key, -4.0, 4.0, (ROWS, SEG, D), jnp.float32)
    return field.astype(jnp.bfloat16)


def draw_seg_keys(key, part):
    key = jax.random.fold_in(key, 2)
    field = jax.random.truncated_normal(key, -4.0, 4.0, (ROWS, SEG, D), jnp.float32)
    return field.astype(jnp.bfloat16)


def draw_mem_keys(key, part):
    key = jax.random.fold_in(key, 3)
    shape = (ROWS, MB_DEV, MEM_BLOCKS // MB_DEV, BLK, D)
    field = jax.random.truncated_normal(key, -4.0, 4.0, shape, jnp.float32)
    return field.astype(jnp.bfloat16)


def draw_pointer(key, part):
    oldest = pointer_slots(key)
    return oldest


def draw_block_ids(key, part):
    oldest = pointer_slots(key)
    key = jax.random.fold_in(key, 4)
    slots = jnp.arange(MEM_BLOCKS, dtype=jnp.int32)
    query_block = jnp.arange(SEG_BLOCKS, dtype=jnp.int32)
    relative = slots[None, None, :] - oldest[:, None, None]
    written = (relative >= 0) & (relative < SEG_BLOCKS)
    allowed = jnp.logical_not(written) | (relative < query_block[None, :, None])
    noise = jax.random.randint(key, (ROWS, SEG_BLOCKS, H, MEM_BLOCKS), 0, 65536)
    ranking = noise * MEM_BLOCKS + slots
    ranking = jnp.where(allowed[:, :, None, :], ranking, -1 - slots)
    chosen = lax.top_k(ranking, TOPK)[1]
    return chosen.astype(jnp.int32)


def levels(own_key, shape, shards, low, largest):
    gain, own = 1.0, jax.random.fold_in(own_key, 6)
    for axis_at, parts in shards:
        heights = jnp.exp(jax.random.uniform(jax.random.fold_in(own, axis_at), (parts,), jnp.float32, low / len(shards), largest / len(shards)))
        gain = gain * jnp.repeat(heights, shape[axis_at] // parts).reshape([-1 if axis == axis_at else 1 for axis in range(len(shape))])
    return gain


def normal_values(rng, extent, width, limit, split=(), held_as=jnp.bfloat16):
    loudness = levels(rng, extent, split, -0.22, 0.18) if split else 1.0
    values = jax.random.normal(rng, extent, jnp.float32) * width * loudness
    return jnp.minimum(jnp.maximum(values, -limit), limit).astype(held_as)


def setup_inputs(seed: int = 0) -> dict:
    keys = jax.random.split(jax.random.key(seed), 10)
    queries = draw_queries(jax.random.fold_in(keys[9], 71), 0)
    seg_keys = draw_seg_keys(jax.random.fold_in(keys[9], 71), 0)
    seg_values = normal_values(keys[2], (ROWS, SEG, D), 1.0, 6.0, ((0, 32), (1, 16)))
    mem_keys = draw_mem_keys(jax.random.fold_in(keys[9], 71), 0)
    mem_values = normal_values(keys[4], (ROWS, MB_DEV, N_MEM, BLK, D), 1.0, 6.0, ((0, 32), (2, 16)))
    block_ids = draw_block_ids(jax.random.fold_in(keys[9], 71), 0)
    pointer = draw_pointer(jax.random.fold_in(keys[9], 71), 0)
    gate_bias = jnp.clip(jax.random.uniform(keys[7], (H,), jnp.float32, -2.0, 2.0) * levels(keys[7], (H,), ((0, 16),), -0.4, 0.0), -2.0, 2.0)
    out_weight = normal_values(keys[8], (D, D), D ** -0.5, 0.125, ((0, 32),))
    return {"queries": queries, "seg_keys": seg_keys, "seg_values": seg_values, "mem_keys": mem_keys, "mem_values": mem_values, "block_ids": block_ids, "pointer": pointer, "gate_bias": gate_bias, "out_weight": out_weight}


def softmax_rows(scores):
    highest = lax.optimization_barrier(jnp.max(scores, axis=-1, keepdims=True))
    expo = jnp.exp(scores - highest)
    return expo / lax.optimization_barrier(jnp.sum(expo, axis=-1, keepdims=True))

def reference(queries, seg_keys, seg_values, mem_keys, mem_values, block_ids, pointer, gate_bias, out_weight):
    score_scale = 1.0 / math.sqrt(HD)
    causal_mask = jnp.arange(SEG)[:, None] >= jnp.arange(SEG)[None, :]

    def one_row(inputs):
        query, key_seg, value_seg, key_mem, value_mem, slot_ids, oldest = inputs
        key_mem = key_mem.reshape(MEM_BLOCKS, BLK, D)
        value_mem = value_mem.reshape(MEM_BLOCKS, BLK, D)
        start = oldest.astype(jnp.int32)
        zero_index = jnp.zeros((), jnp.int32)
        key_mem = lax.dynamic_update_slice(key_mem, key_seg.reshape(SEG_BLOCKS, BLK, D), (start, zero_index, zero_index))
        value_mem = lax.dynamic_update_slice(value_mem, value_seg.reshape(SEG_BLOCKS, BLK, D), (start, zero_index, zero_index))
        query_heads = query.reshape(SEG, H, HD).transpose(1, 0, 2)
        key_heads = key_seg.reshape(SEG, H, HD).transpose(1, 0, 2)
        value_heads = value_seg.reshape(SEG, H, HD).transpose(1, 0, 2)
        memk_heads = key_mem.reshape(MEM_BLOCKS, BLK, H, HD).transpose(2, 0, 1, 3)
        memv_heads = value_mem.reshape(MEM_BLOCKS, BLK, H, HD).transpose(2, 0, 1, 3)
        slot_heads = slot_ids.transpose(1, 0, 2)

        def one_head(head_inputs):
            query_h, key_h, value_h, memk_h, memv_h, slots_h = head_inputs
            scores = jnp.dot(query_h, key_h.T, preferred_element_type=jnp.float32) * score_scale
            scores = jnp.where(causal_mask, scores, -1e+30)
            weights = softmax_rows(scores).astype(jnp.bfloat16)
            local_out = jnp.dot(weights, value_h, preferred_element_type=jnp.float32)
            query_blocks = query_h.reshape(SEG_BLOCKS, BLK, HD).astype(jnp.float32)
            fetched_k = memk_h[slots_h].reshape(SEG_BLOCKS, TOPK * BLK, HD).astype(jnp.float32)
            fetched_v = memv_h[slots_h].reshape(SEG_BLOCKS, TOPK * BLK, HD).astype(jnp.float32)
            mem_scores = jnp.einsum('qtd,qkd->qtk', query_blocks, fetched_k) * score_scale
            mem_weights = lax.optimization_barrier(softmax_rows(mem_scores).astype(jnp.bfloat16)).astype(jnp.float32)
            memory_out = jnp.einsum('qtk,qkd->qtd', mem_weights, fetched_v).reshape(SEG, HD)
            return (local_out, memory_out)
        local_all, memory_all = lax.map(one_head, (query_heads, key_heads, value_heads, memk_heads, memv_heads, slot_heads))
        gates = jax.nn.sigmoid(gate_bias)[:, None, None]
        attended = (gates * memory_all + (1.0 - gates) * local_all).astype(jnp.bfloat16)
        attended = attended.transpose(1, 0, 2).reshape(SEG, D)
        return jnp.dot(attended, out_weight, preferred_element_type=jnp.float32).astype(jnp.bfloat16)
    return lax.map(one_row, (queries, seg_keys, seg_values, mem_keys, mem_values, block_ids, pointer))
```

```python
import functools
import math

import jax
import jax.numpy as jnp
from jax import lax
from jax.experimental import pallas as pl
from jax.experimental.pallas import tpu as pltpu
from jax.sharding import PartitionSpec as P

HD = 128
BLK = 128
N = 16
SEG = N * BLK
PAIR = 2 * BLK
WIDE = 4 * BLK
LOW = -1e30
SCALE = math.log2(math.e) / math.sqrt(HD)
MESH = pl.DeviceIdType.MESH

OFFSETS = [8] + [x for d in range(7, 0, -1) for x in (d, N - d)]


def nt_dot(a, b):
    return lax.dot_general(a, b, (((1,), (1,)), ((), ())), preferred_element_type=jnp.float32)


def nn_dot(a, b):
    return jnp.dot(a, b, preferred_element_type=jnp.float32)


def rows_of(index, size):
    return pl.ds(pl.multiple_of(index * size, size), size)


def kernel(
    dims,
    pointer_ref, gate_ref, ids_ref, q_in, k_in, v_in, mk_in, mv_in, w_in, out_ref,
    qb, kb, vb, mkb, mvb, mk_both, mv_both, mk_old, mv_old, bias, scores,
    p_local, p_seg, p_old, base, mem_num, mem_den, sent, heads, wb, total,
    send_sem, recv_sem, own_sem, w_send, w_recv,
):
    ys, xs, cs = dims
    z = lax.axis_index("mem")
    dp = lax.axis_index("dp")
    core = lax.rem(dp, cs)
    x = lax.rem(dp // cs, xs)
    y = dp // (cs * xs)

    def at_z(offset):
        return lax.rem(z + offset, N)

    x_peers = [(y * xs + lax.rem(x + d, xs)) * cs + core for d in range(1, xs)]
    y_peers = [(lax.rem(y + d, ys) * xs + x) * cs + core for d in range(1, ys)]
    sibling = (y * xs + x) * cs + (1 - core)
    plane = x_peers + y_peers + [sibling]

    own = [
        pltpu.make_async_copy(mk_in.at[0, :, 0], mk_both, own_sem.at[0]),
        pltpu.make_async_copy(mv_in.at[0, :, 0], mv_both, own_sem.at[1]),
        pltpu.make_async_copy(q_in.at[0, :, rows_of(z, HD)], qb.at[rows_of(z, BLK)], own_sem.at[2]),
        pltpu.make_async_copy(k_in.at[0, :, rows_of(z, HD)], kb.at[rows_of(z, BLK)], own_sem.at[3]),
        pltpu.make_async_copy(v_in.at[0, :, rows_of(z, HD)], vb.at[rows_of(z, BLK)], own_sem.at[4]),
        pltpu.make_async_copy(w_in, wb.at[y * xs + x, core], own_sem.at[5]),
    ]
    for copy in own:
        copy.start()

    barrier = pltpu.get_barrier_semaphore()
    for o in OFFSETS:
        pl.semaphore_signal(barrier, inc=1, device_id={"mem": at_z(o)}, device_id_type=MESH)
    for peer in plane:
        pl.semaphore_signal(barrier, inc=1, device_id={"dp": peer}, device_id_type=MESH)
    pl.semaphore_wait(barrier, len(OFFSETS) + len(plane))

    def head_copy(a, o, src, dst):
        return pltpu.make_async_remote_copy(
            src_ref=src, dst_ref=dst, send_sem=send_sem.at[a, o], recv_sem=recv_sem.at[a, o],
            device_id={"mem": at_z(o)}, device_id_type=MESH,
        )

    def scatter(a, src, dst):
        copies = [
            head_copy(a, o, src.at[:, rows_of(at_z(o), HD)], dst.at[rows_of(z, BLK)])
            for o in OFFSETS
        ]
        for copy in copies:
            copy.start()
        return copies

    def w_copy(n, src, dst, peer):
        return pltpu.make_async_remote_copy(
            src_ref=src, dst_ref=dst, send_sem=w_send.at[n], recv_sem=w_recv.at[n],
            device_id={"dp": peer}, device_id_type=MESH,
        )

    w_first = [
        w_copy(n, w_in, wb.at[y * xs + x, core], peer) for n, peer in enumerate(x_peers)
    ]
    for copy in w_first:
        copy.start()
    q_copies = scatter(0, q_in.at[0], qb)
    k_copies = scatter(1, k_in.at[0], kb)

    pointer = pointer_ref[0]
    column = 1 - pointer // N

    def keep_old(both, old, copy):
        copy.wait()

        def step(r, _):
            old[rows_of(r, 16), :] = both[column, rows_of(r, 16), :]
            return 0

        lax.fori_loop(0, BLK // 16, step, 0)

    keep_old(mk_both, mk_old, own[0])
    mk_copies = scatter(2, mk_old, mkb)
    v_copies = scatter(3, v_in.at[0], vb)
    keep_old(mv_both, mv_old, own[1])
    mv_copies = scatter(4, mv_old, mvb)
    mkb[rows_of(z, BLK), :] = mk_old[:, rows_of(z, HD)]
    mvb[rows_of(z, BLK), :] = mv_old[:, rows_of(z, HD)]

    place = (ids_ref[0, :, 0, :] + pointer) & (2 * N - 1)
    block_of = lax.broadcasted_iota(jnp.int32, (N, WIDE), 1) // BLK
    for c in range(2 * N * BLK // WIDE):
        picked = jnp.full((N, WIDE), LOW, jnp.float32)
        for t in range(N):
            hit = (block_of + c * (WIDE // BLK)) == place[:, t : t + 1]
            picked = jnp.where(hit, 0.0, picked)
        bias[:, c * WIDE : (c + 1) * WIDE] = picked

    own[5].wait()
    for copy in w_first:
        copy.wait_recv()
    mine = wb.at[pl.ds(y * xs, xs), core]
    w_second = [w_copy(xs - 1 + n, mine, mine, peer) for n, peer in enumerate(y_peers)]
    for copy in w_second:
        copy.start()

    own[2].wait()
    own[3].wait()
    for copy in q_copies + k_copies:
        copy.wait_recv()

    def lane_max(m, s):
        for c in range(s.shape[1] // 128):
            m = jnp.maximum(m, s[:, c * 128 : (c + 1) * 128])
        return m

    def local_pair(i, _):
        q = qb[rows_of(i, PAIR), :]

        def first(j, m):
            s = nt_dot(q, kb[rows_of(j, PAIR), :]) * SCALE
            scores[:, rows_of(j, PAIR)] = s
            return lane_max(m, s)

        m = lax.fori_loop(0, i, first, jnp.full((PAIR, 128), LOW, jnp.float32))
        s = nt_dot(q, kb[rows_of(i, PAIR), :]) * SCALE
        row = lax.broadcasted_iota(jnp.int32, (PAIR, PAIR), 0)
        col = lax.broadcasted_iota(jnp.int32, (PAIR, PAIR), 1)
        s = jnp.where(row >= col, s, LOW)
        highest = jnp.max(lane_max(m, s), axis=1, keepdims=True)
        p_local[rows_of(i, PAIR), rows_of(i, PAIR)] = jnp.exp2(s - highest).astype(jnp.bfloat16)

        def second(j, _):
            p = jnp.exp2(scores[:, rows_of(j, PAIR)] - highest)
            p_local[rows_of(i, PAIR), rows_of(j, PAIR)] = p.astype(jnp.bfloat16)
            return 0

        lax.fori_loop(0, i, second, 0)
        return 0

    lax.fori_loop(0, N // 2, local_pair, 0)

    for copy in w_second:
        copy.wait_recv()
    half = wb.at[:, core]
    w_third = w_copy(xs + ys - 2, half, half, sibling)
    w_third.start()

    for copy in mk_copies:
        copy.wait_recv()

    def memory_pair(i, _):
        q = qb[rows_of(i, PAIR), :]

        def biased(s, at):
            return jnp.concatenate(
                [
                    s[:BLK] + bias[pl.ds(2 * i, 1), at],
                    s[BLK:] + bias[pl.ds(2 * i + 1, 1), at],
                ],
                axis=0,
            )

        m = jnp.full((PAIR, 128), LOW, jnp.float32)
        for c in range(SEG // WIDE):
            s = nt_dot(q, mkb[c * WIDE : (c + 1) * WIDE, :]) * SCALE
            s = biased(s, slice(SEG + c * WIDE, SEG + (c + 1) * WIDE))
            scores[:, SEG + c * WIDE : SEG + (c + 1) * WIDE] = s
            m = lane_max(m, s)

        def first(j, m):
            s = biased(nt_dot(q, kb[rows_of(j, PAIR), :]) * SCALE, rows_of(j, PAIR))
            scores[:, rows_of(j, PAIR)] = s
            return lane_max(m, s)

        m = lax.fori_loop(0, i + 1, first, m)
        highest = jnp.max(m, axis=1, keepdims=True)
        for c in range(SEG // WIDE):
            p = jnp.exp2(scores[:, SEG + c * WIDE : SEG + (c + 1) * WIDE] - highest)
            p_old[rows_of(i, PAIR), c * WIDE : (c + 1) * WIDE] = p.astype(jnp.bfloat16)

        def second(j, _):
            p = jnp.exp2(scores[:, rows_of(j, PAIR)] - highest)
            p_seg[rows_of(i, PAIR), rows_of(j, PAIR)] = p.astype(jnp.bfloat16)
            return 0

        lax.fori_loop(0, i + 1, second, 0)
        return 0

    lax.fori_loop(0, N // 2, memory_pair, 0)

    own[4].wait()
    for copy in v_copies:
        copy.wait_recv()
    gate = 1.0 / (1.0 + jnp.exp(jnp.full((8, 128), -gate_ref[0], jnp.float32)))[:1]
    ones = jnp.ones((PAIR, 128), jnp.bfloat16)

    def value_pair(i, _):
        def step(j, acc):
            values = jnp.concatenate([vb[rows_of(j, PAIR), :], ones], axis=1)
            p = jnp.concatenate(
                [
                    p_local[rows_of(i, PAIR), rows_of(j, PAIR)],
                    p_seg[rows_of(i, PAIR), rows_of(j, PAIR)],
                ],
                axis=0,
            )
            return acc + nn_dot(p, values)

        acc = lax.fori_loop(0, i + 1, step, jnp.zeros((2 * PAIR, PAIR), jnp.float32))
        base[rows_of(i, PAIR), :] = (1.0 - gate) * (acc[:PAIR, :128] / acc[:PAIR, 128:])
        mem_num[rows_of(i, PAIR), :] = acc[PAIR:, :128]
        mem_den[rows_of(i, PAIR), :] = acc[PAIR:, 128:]
        return 0

    lax.fori_loop(0, N // 2, value_pair, 0)

    for copy in mv_copies:
        copy.wait_recv()

    def finish(o):
        i = at_z(o)
        rows = rows_of(i, BLK)
        values = jnp.concatenate([mvb[...], jnp.ones((SEG, 128), jnp.bfloat16)], axis=1)
        got = nn_dot(p_old[rows, :], values)
        memory = (got[:, :128] + mem_num[rows, :]) / (got[:, 128:] + mem_den[rows, :])
        return (gate * memory + base[rows, :]).astype(jnp.bfloat16)

    out_copies = []
    for n, o in enumerate(OFFSETS):
        sent[n] = finish(o)
        copy = head_copy(5, o, sent.at[n], heads.at[z])
        copy.start()
        out_copies.append(copy)
    heads[z] = finish(0)

    w_third.wait_recv()

    def weights(h):
        return wb[h].reshape(HD, wb.shape[-1])

    total[...] = nn_dot(heads[z], weights(z))
    for n, o in enumerate(OFFSETS):
        out_copies[n].wait_recv()
        h = at_z(N - o)
        if n < len(OFFSETS) - 1:
            total[...] += nn_dot(heads[h], weights(h))
        else:
            out_ref[0] = (total[...] + nn_dot(heads[h], weights(h))).astype(jnp.bfloat16)

    for copy in w_first + w_second + [w_third]:
        copy.wait_send()
    for copy in q_copies + k_copies + mk_copies + v_copies + mv_copies + out_copies:
        copy.wait_send()


def local(
    dims,
    queries, seg_keys, seg_values, mem_keys, mem_values, block_ids, pointer, gate_bias, out_weight,
):
    width = queries.shape[2]
    ys, xs, cs = dims
    bf16, f32 = jnp.bfloat16, jnp.float32
    vmem, smem, hbm = (
        pl.BlockSpec(memory_space=pltpu.VMEM),
        pl.BlockSpec(memory_space=pltpu.SMEM),
        pl.BlockSpec(memory_space=pl.ANY),
    )
    n_plane = xs + ys - 1
    return pl.pallas_call(
        functools.partial(kernel, dims),
        out_shape=jax.ShapeDtypeStruct(queries.shape, bf16),
        in_specs=[smem, smem, vmem, hbm, hbm, hbm, hbm, hbm, hbm],
        out_specs=vmem,
        scratch_shapes=[
            *[pltpu.VMEM((SEG, HD), bf16) for _ in range(5)],
            pltpu.VMEM((2, BLK, width), bf16),
            pltpu.VMEM((2, BLK, width), bf16),
            pltpu.VMEM((BLK, width), bf16),
            pltpu.VMEM((BLK, width), bf16),
            pltpu.VMEM((N, 2 * SEG), f32),
            pltpu.VMEM((PAIR, 2 * SEG), f32),
            pltpu.VMEM((SEG, SEG), bf16),
            pltpu.VMEM((SEG, SEG), bf16),
            pltpu.VMEM((SEG, SEG), bf16),
            pltpu.VMEM((SEG, HD), f32),
            pltpu.VMEM((SEG, HD), f32),
            pltpu.VMEM((SEG, HD), f32),
            pltpu.VMEM((N - 1, BLK, HD), bf16),
            pltpu.VMEM((N, BLK, HD), bf16),
            pltpu.VMEM((ys * xs, cs, *out_weight.shape), bf16),
            pltpu.VMEM((BLK, width), f32),
            pltpu.SemaphoreType.DMA((6, N)),
            pltpu.SemaphoreType.DMA((6, N)),
            pltpu.SemaphoreType.DMA((6,)),
            pltpu.SemaphoreType.DMA((n_plane,)),
            pltpu.SemaphoreType.DMA((n_plane,)),
        ],
        compiler_params=pltpu.CompilerParams(
            collective_id=0, has_side_effects=True, vmem_limit_bytes=60 * 1024 * 1024
        ),
        cost_estimate=pl.CostEstimate(
            flops=5_000_000_000, bytes_accessed=5_000_000, transcendentals=9_000_000
        ),
    )(pointer, gate_bias, block_ids, queries, seg_keys, seg_values, mem_keys, mem_values, out_weight)


def solution(mesh):
    dims = (4, 4, 2)
    in_specs = (
        P("dp", "mem", None),
        P("dp", "mem", None),
        P("dp", "mem", None),
        P("dp", None, "mem", None, None),
        P("dp", None, "mem", None, None),
        P("dp", None, "mem", None),
        P("dp"),
        P("mem"),
        P("dp", None),
    )
    return jax.shard_map(
        functools.partial(local, dims), mesh=mesh, in_specs=in_specs,
        out_specs=P("dp", "mem", None), check_vma=False,
    )
```

```python
import functools
import math

import jax
import jax.numpy as jnp
from jax import lax
from jax.experimental import pallas as pl
from jax.experimental.pallas import tpu as pltpu
from jax.sharding import PartitionSpec as P

HD = 128
BLK = 128
N = 16
SEG = N * BLK
PAIR = 2 * BLK
WIDE = 4 * BLK
LOW = -1e30
SCALE = math.log2(math.e) / math.sqrt(HD)
MESH = pl.DeviceIdType.MESH

OFFSETS = [8] + [x for d in range(7, 0, -1) for x in (d, N - d)]


def nt_dot(a, b):
    return lax.dot_general(a, b, (((1,), (1,)), ((), ())), preferred_element_type=jnp.float32)


def nn_dot(a, b):
    return jnp.dot(a, b, preferred_element_type=jnp.float32)


def rows_of(index, size):
    return pl.ds(pl.multiple_of(index * size, size), size)


def kernel(
    dims,
    pointer_in, gate_in, ids_in, q_in, k_in, v_in, mk_in, mv_in, w_in, out_ref,
    pointer_ref, gate_ref, ids_ref, qb, kb, vb, mkb, mvb, mk_both, mv_both, mk_old, mv_old, bias, scores,
    p_local, p_seg, p_old, base, mem_num, mem_den, sent, heads, wb, total,
    send_sem, recv_sem, own_sem, w_send, w_recv,
):
    ys, xs, cs = dims
    z = lax.axis_index("mem")
    dp = lax.axis_index("dp")
    core = lax.rem(dp, cs)
    x = lax.rem(dp // cs, xs)
    y = dp // (cs * xs)

    def at_z(offset):
        return lax.rem(z + offset, N)

    x_peers = [(y * xs + lax.rem(x + d, xs)) * cs + core for d in range(1, xs)]
    y_peers = [(lax.rem(y + d, ys) * xs + x) * cs + core for d in range(1, ys)]
    sibling = (y * xs + x) * cs + (1 - core)
    plane = x_peers + y_peers + [sibling]

    own = [
        pltpu.make_async_copy(mk_in.at[0, :, 0], mk_both, own_sem.at[0]),
        pltpu.make_async_copy(mv_in.at[0, :, 0], mv_both, own_sem.at[1]),
        pltpu.make_async_copy(q_in.at[0, :, rows_of(z, HD)], qb.at[rows_of(z, BLK)], own_sem.at[2]),
        pltpu.make_async_copy(k_in.at[0, :, rows_of(z, HD)], kb.at[rows_of(z, BLK)], own_sem.at[3]),
        pltpu.make_async_copy(v_in.at[0, :, rows_of(z, HD)], vb.at[rows_of(z, BLK)], own_sem.at[4]),
        pltpu.make_async_copy(w_in, wb.at[y * xs + x, core], own_sem.at[5]),
        pltpu.make_async_copy(pointer_in, pointer_ref, own_sem.at[6]),
        pltpu.make_async_copy(gate_in, gate_ref, own_sem.at[7]),
        pltpu.make_async_copy(ids_in, ids_ref, own_sem.at[8]),
    ]
    for copy in own:
        copy.start()

    barrier = pltpu.get_barrier_semaphore()
    for o in OFFSETS:
        pl.semaphore_signal(barrier, inc=1, device_id={"mem": at_z(o)}, device_id_type=MESH)
    for peer in plane:
        pl.semaphore_signal(barrier, inc=1, device_id={"dp": peer}, device_id_type=MESH)
    pl.semaphore_wait(barrier, len(OFFSETS) + len(plane))

    def head_copy(a, o, src, dst):
        return pltpu.make_async_remote_copy(
            src_ref=src, dst_ref=dst, send_sem=send_sem.at[a, o], recv_sem=recv_sem.at[a, o],
            device_id={"mem": at_z(o)}, device_id_type=MESH,
        )

    def scatter(a, src, dst):
        copies = [
            head_copy(a, o, src.at[:, rows_of(at_z(o), HD)], dst.at[rows_of(z, BLK)])
            for o in OFFSETS
        ]
        for copy in copies:
            copy.start()
        return copies

    def w_copy(n, src, dst, peer):
        return pltpu.make_async_remote_copy(
            src_ref=src, dst_ref=dst, send_sem=w_send.at[n], recv_sem=w_recv.at[n],
            device_id={"dp": peer}, device_id_type=MESH,
        )

    w_first = [
        w_copy(n, w_in, wb.at[y * xs + x, core], peer) for n, peer in enumerate(x_peers)
    ]
    for copy in w_first:
        copy.start()
    q_copies = scatter(0, q_in.at[0], qb)
    k_copies = scatter(1, k_in.at[0], kb)

    own[6].wait()
    pointer = pointer_ref[0]
    column = 1 - pointer // N

    def keep_old(both, old, copy):
        copy.wait()

        def step(r, _):
            old[rows_of(r, 16), :] = both[column, rows_of(r, 16), :]
            return 0

        lax.fori_loop(0, BLK // 16, step, 0)

    keep_old(mk_both, mk_old, own[0])
    mk_copies = scatter(2, mk_old, mkb)
    v_copies = scatter(3, v_in.at[0], vb)
    keep_old(mv_both, mv_old, own[1])
    mv_copies = scatter(4, mv_old, mvb)
    mkb[rows_of(z, BLK), :] = mk_old[:, rows_of(z, HD)]
    mvb[rows_of(z, BLK), :] = mv_old[:, rows_of(z, HD)]

    own[8].wait()
    place = (ids_ref[0, :, 0, :] + pointer) & (2 * N - 1)
    block_of = lax.broadcasted_iota(jnp.int32, (N, WIDE), 1) // BLK
    for c in range(2 * N * BLK // WIDE):
        picked = jnp.full((N, WIDE), LOW, jnp.float32)
        for t in range(N):
            hit = (block_of + c * (WIDE // BLK)) == place[:, t : t + 1]
            picked = jnp.where(hit, 0.0, picked)
        bias[:, c * WIDE : (c + 1) * WIDE] = picked

    own[5].wait()
    for copy in w_first:
        copy.wait_recv()
    mine = wb.at[pl.ds(y * xs, xs), core]
    w_second = [w_copy(xs - 1 + n, mine, mine, peer) for n, peer in enumerate(y_peers)]
    for copy in w_second:
        copy.start()

    own[2].wait()
    own[3].wait()
    for copy in q_copies + k_copies:
        copy.wait_recv()

    def lane_max(m, s):
        for c in range(s.shape[1] // 128):
            m = jnp.maximum(m, s[:, c * 128 : (c + 1) * 128])
        return m

    def local_pair(i, _):
        q = qb[rows_of(i, PAIR), :]

        def first(j, m):
            s = nt_dot(q, kb[rows_of(j, PAIR), :]) * SCALE
            scores[:, rows_of(j, PAIR)] = s
            return lane_max(m, s)

        m = lax.fori_loop(0, i, first, jnp.full((PAIR, 128), LOW, jnp.float32))
        s = nt_dot(q, kb[rows_of(i, PAIR), :]) * SCALE
        row = lax.broadcasted_iota(jnp.int32, (PAIR, PAIR), 0)
        col = lax.broadcasted_iota(jnp.int32, (PAIR, PAIR), 1)
        s = jnp.where(row >= col, s, LOW)
        highest = jnp.max(lane_max(m, s), axis=1, keepdims=True)
        p_local[rows_of(i, PAIR), rows_of(i, PAIR)] = jnp.exp2(s - highest).astype(jnp.bfloat16)

        def second(j, _):
            p = jnp.exp2(scores[:, rows_of(j, PAIR)] - highest)
            p_local[rows_of(i, PAIR), rows_of(j, PAIR)] = p.astype(jnp.bfloat16)
            return 0

        lax.fori_loop(0, i, second, 0)
        return 0

    lax.fori_loop(0, N // 2, local_pair, 0)

    for copy in w_second:
        copy.wait_recv()
    half = wb.at[:, core]
    w_third = w_copy(xs + ys - 2, half, half, sibling)
    w_third.start()

    for copy in mk_copies:
        copy.wait_recv()

    def memory_pair(i, _):
        q = qb[rows_of(i, PAIR), :]

        def biased(s, at):
            return jnp.concatenate(
                [
                    s[:BLK] + bias[pl.ds(2 * i, 1), at],
                    s[BLK:] + bias[pl.ds(2 * i + 1, 1), at],
                ],
                axis=0,
            )

        m = jnp.full((PAIR, 128), LOW, jnp.float32)
        for c in range(SEG // WIDE):
            s = nt_dot(q, mkb[c * WIDE : (c + 1) * WIDE, :]) * SCALE
            s = biased(s, slice(SEG + c * WIDE, SEG + (c + 1) * WIDE))
            scores[:, SEG + c * WIDE : SEG + (c + 1) * WIDE] = s
            m = lane_max(m, s)

        def first(j, m):
            s = biased(nt_dot(q, kb[rows_of(j, PAIR), :]) * SCALE, rows_of(j, PAIR))
            scores[:, rows_of(j, PAIR)] = s
            return lane_max(m, s)

        m = lax.fori_loop(0, i + 1, first, m)
        highest = jnp.max(m, axis=1, keepdims=True)
        for c in range(SEG // WIDE):
            p = jnp.exp2(scores[:, SEG + c * WIDE : SEG + (c + 1) * WIDE] - highest)
            p_old[rows_of(i, PAIR), c * WIDE : (c + 1) * WIDE] = p.astype(jnp.bfloat16)

        def second(j, _):
            p = jnp.exp2(scores[:, rows_of(j, PAIR)] - highest)
            p_seg[rows_of(i, PAIR), rows_of(j, PAIR)] = p.astype(jnp.bfloat16)
            return 0

        lax.fori_loop(0, i + 1, second, 0)
        return 0

    lax.fori_loop(0, N // 2, memory_pair, 0)

    own[4].wait()
    for copy in v_copies:
        copy.wait_recv()
    own[7].wait()
    gate = 1.0 / (1.0 + jnp.exp(jnp.full((8, 128), -gate_ref[0], jnp.float32)))[:1]
    ones = jnp.ones((PAIR, 128), jnp.bfloat16)

    def value_pair(i, _):
        def step(j, acc):
            values = jnp.concatenate([vb[rows_of(j, PAIR), :], ones], axis=1)
            p = jnp.concatenate(
                [
                    p_local[rows_of(i, PAIR), rows_of(j, PAIR)],
                    p_seg[rows_of(i, PAIR), rows_of(j, PAIR)],
                ],
                axis=0,
            )
            return acc + nn_dot(p, values)

        acc = lax.fori_loop(0, i + 1, step, jnp.zeros((2 * PAIR, PAIR), jnp.float32))
        base[rows_of(i, PAIR), :] = (1.0 - gate) * (acc[:PAIR, :128] / acc[:PAIR, 128:])
        mem_num[rows_of(i, PAIR), :] = acc[PAIR:, :128]
        mem_den[rows_of(i, PAIR), :] = acc[PAIR:, 128:]
        return 0

    lax.fori_loop(0, N // 2, value_pair, 0)

    for copy in mv_copies:
        copy.wait_recv()

    def finish(o):
        i = at_z(o)
        rows = rows_of(i, BLK)
        values = jnp.concatenate([mvb[...], jnp.ones((SEG, 128), jnp.bfloat16)], axis=1)
        got = nn_dot(p_old[rows, :], values)
        memory = (got[:, :128] + mem_num[rows, :]) / (got[:, 128:] + mem_den[rows, :])
        return (gate * memory + base[rows, :]).astype(jnp.bfloat16)

    out_copies = []
    for n, o in enumerate(OFFSETS):
        sent[n] = finish(o)
        copy = head_copy(5, o, sent.at[n], heads.at[z])
        copy.start()
        out_copies.append(copy)
    heads[z] = finish(0)

    w_third.wait_recv()

    def weights(h):
        return wb[h].reshape(HD, wb.shape[-1])

    total[...] = nn_dot(heads[z], weights(z))
    for n, o in enumerate(OFFSETS):
        out_copies[n].wait_recv()
        h = at_z(N - o)
        if n < len(OFFSETS) - 1:
            total[...] += nn_dot(heads[h], weights(h))
        else:
            out_ref[0] = (total[...] + nn_dot(heads[h], weights(h))).astype(jnp.bfloat16)

    for copy in w_first + w_second + [w_third]:
        copy.wait_send()
    for copy in q_copies + k_copies + mk_copies + v_copies + mv_copies + out_copies:
        copy.wait_send()


def local(
    dims,
    queries, seg_keys, seg_values, mem_keys, mem_values, block_ids, pointer, gate_bias, out_weight,
):
    width = queries.shape[2]
    ys, xs, cs = dims
    bf16, f32 = jnp.bfloat16, jnp.float32
    hbm = pl.BlockSpec(memory_space=pltpu.HBM)
    n_plane = xs + ys - 1
    return pl.pallas_call(
        functools.partial(kernel, dims),
        out_shape=pltpu.VMEM(queries.shape, bf16),
        in_specs=[hbm] * 9,
        out_specs=pl.BlockSpec(memory_space=pltpu.VMEM),
        scratch_shapes=[
            pltpu.SMEM(pointer.shape, jnp.int32),
            pltpu.SMEM(gate_bias.shape, f32),
            pltpu.VMEM(block_ids.shape, jnp.int32),
            *[pltpu.VMEM((SEG, HD), bf16) for _ in range(5)],
            pltpu.VMEM((2, BLK, width), bf16),
            pltpu.VMEM((2, BLK, width), bf16),
            pltpu.VMEM((BLK, width), bf16),
            pltpu.VMEM((BLK, width), bf16),
            pltpu.VMEM((N, 2 * SEG), f32),
            pltpu.VMEM((PAIR, 2 * SEG), f32),
            pltpu.VMEM((SEG, SEG), bf16),
            pltpu.VMEM((SEG, SEG), bf16),
            pltpu.VMEM((SEG, SEG), bf16),
            pltpu.VMEM((SEG, HD), f32),
            pltpu.VMEM((SEG, HD), f32),
            pltpu.VMEM((SEG, HD), f32),
            pltpu.VMEM((N - 1, BLK, HD), bf16),
            pltpu.VMEM((N, BLK, HD), bf16),
            pltpu.VMEM((ys * xs, cs, *out_weight.shape), bf16),
            pltpu.VMEM((BLK, width), f32),
            pltpu.SemaphoreType.DMA((6, N)),
            pltpu.SemaphoreType.DMA((6, N)),
            pltpu.SemaphoreType.DMA((9,)),
            pltpu.SemaphoreType.DMA((n_plane,)),
            pltpu.SemaphoreType.DMA((n_plane,)),
        ],
        compiler_params=pltpu.CompilerParams(
            collective_id=0, has_side_effects=True, vmem_limit_bytes=60 * 1024 * 1024
        ),
        cost_estimate=pl.CostEstimate(
            flops=5_000_000_000, bytes_accessed=5_000_000, transcendentals=9_000_000
        ),
    )(pointer, gate_bias, block_ids, queries, seg_keys, seg_values, mem_keys, mem_values, out_weight)


def solution(mesh):
    dims = (4, 4, 2)
    in_specs = (
        P("dp", "mem", None),
        P("dp", "mem", None),
        P("dp", "mem", None),
        P("dp", None, "mem", None, None),
        P("dp", None, "mem", None, None),
        P("dp", None, "mem", None),
        P("dp"),
        P("mem"),
        P("dp", None),
    )
    return jax.shard_map(
        functools.partial(local, dims), mesh=mesh, in_specs=in_specs,
        out_specs=P("dp", "mem", None), check_vma=False,
    )
```

```python
import functools
import math

import jax
import jax.numpy as jnp
from jax import lax
from jax.experimental import pallas as pl
from jax.experimental.pallas import tpu as pltpu
from jax.sharding import PartitionSpec as P

HD = 128
BLK = 128
N = 16
HALF = N // 2
SEG = N * BLK
KEYS = HALF * BLK
PAIR = 2 * BLK
WIDE = 4 * BLK
LOW = -1e30
LOG2E = math.log2(math.e)
SCALE = LOG2E / math.sqrt(HD)
MESH = pl.DeviceIdType.MESH

GAP = 3
LEFT = 6
ROLES = (0, 1)


def offset(role, w):
    return LEFT - w if role == 0 else LEFT + GAP - HALF - w


def head_shift(role):
    return 0 if role == 0 else -GAP


FAR_FIRST = sorted(
    [(role, w) for role in ROLES for w in range(HALF) if offset(role, w)],
    key=lambda rw: -abs(offset(*rw)),
)
OWN = [(role, w) for role in ROLES for w in range(HALF) if offset(role, w) == 0]
PEERS = sorted({offset(*rw) for rw in FAR_FIRST} | {GAP, -GAP})


def nt_dot(a, b):
    return lax.dot_general(a, b, (((1,), (1,)), ((), ())), preferred_element_type=jnp.float32)


def nn_dot(a, b):
    return jnp.dot(a, b, preferred_element_type=jnp.float32)


def rows_of(index, size):
    return pl.ds(pl.multiple_of(index * size, size), size)


def log2(x):
    return jnp.log(x) * LOG2E


def join(a, b):
    m = jnp.maximum(a, b)
    return m + log2(jnp.exp2(a - m) + jnp.exp2(b - m))


def kernel(
    dims,
    pointer_in, gate_in, ids_in, q_in, k_in, v_in, mk_in, mv_in, w_in, out_ref,
    pointer_ref, gate_ref, ids, gates, qb, kb, vb, mkb, mvb, mk_both, mv_both, mk_old, mv_old,
    bias, scores, p_loc, p_seg, p_old, parts, stats, lines, lse_out, lse_in, part_out, part_in,
    sent, heads, wb, total,
    send_sem, recv_sem, out_send, out_recv, part_send, part_recv, pass_send, pass_recv,
    own_sem, w_send, w_recv,
):
    ys, xs, cs = dims
    z = lax.axis_index("mem")
    dp = lax.axis_index("dp")
    core = lax.rem(dp, cs)
    x = lax.rem(dp // cs, xs)
    y = dp // (cs * xs)

    def at_z(o):
        return lax.rem(z + (o + N), N)

    x_peers = [(y * xs + lax.rem(x + d, xs)) * cs + core for d in range(1, xs)]
    y_peers = [(lax.rem(y + d, ys) * xs + x) * cs + core for d in range(1, ys)]
    sibling = (y * xs + x) * cs + (1 - core)
    plane = x_peers + y_peers + [sibling]

    singles = [
        pltpu.make_async_copy(mk_in.at[0, :, 0], mk_both, own_sem.at[0]),
        pltpu.make_async_copy(mv_in.at[0, :, 0], mv_both, own_sem.at[1]),
        pltpu.make_async_copy(w_in, wb.at[y * xs + x, core], own_sem.at[2]),
        pltpu.make_async_copy(pointer_in, pointer_ref, own_sem.at[3]),
        pltpu.make_async_copy(gate_in, gate_ref, own_sem.at[4]),
        pltpu.make_async_copy(ids_in.at[0, :, 0], ids.at[0], own_sem.at[5]),
    ]

    def own_copies(n, src, dst, q):
        copies = []
        for role, w in OWN:
            row = w + (HALF * role if q else 0)
            copies.append(
                pltpu.make_async_copy(
                    src.at[0, :, rows_of(at_z(head_shift(role)), HD)],
                    dst.at[role, row * BLK : (row + 1) * BLK],
                    own_sem.at[n + role],
                )
            )
        return copies

    own_q, own_k = own_copies(6, q_in, qb, True), own_copies(8, k_in, kb, False)
    own_v = own_copies(10, v_in, vb, False)
    for copy in singles + own_q + own_k + own_v:
        copy.start()

    barrier = pltpu.get_barrier_semaphore()
    for o in PEERS:
        pl.semaphore_signal(barrier, inc=1, device_id={"mem": at_z(o)}, device_id_type=MESH)
    for peer in plane:
        pl.semaphore_signal(barrier, inc=1, device_id={"dp": peer}, device_id_type=MESH)
    pl.semaphore_wait(barrier, len(PEERS) + len(plane))

    def along_z(o, src, dst, sent_to, got):
        return pltpu.make_async_remote_copy(
            src_ref=src, dst_ref=dst, send_sem=sent_to, recv_sem=got,
            device_id={"mem": at_z(o)}, device_id_type=MESH,
        )

    def scatter(a, src, dst, q=False):
        copies = []
        for role, w in FAR_FIRST:
            o = offset(role, w)
            row = w + (HALF * role if q else 0)
            copy = along_z(
                o, src.at[:, rows_of(at_z(o + head_shift(role)), HD)],
                dst.at[role, row * BLK : (row + 1) * BLK],
                send_sem.at[a, role, w], recv_sem.at[a, role, w],
            )
            copy.start()
            copies.append(copy)
        return copies

    def w_copy(n, src, dst, peer):
        return pltpu.make_async_remote_copy(
            src_ref=src, dst_ref=dst, send_sem=w_send.at[n], recv_sem=w_recv.at[n],
            device_id={"dp": peer}, device_id_type=MESH,
        )

    w_first = [
        w_copy(n, w_in, wb.at[y * xs + x, core], peer) for n, peer in enumerate(x_peers)
    ]
    for copy in w_first:
        copy.start()
    q_copies = scatter(0, q_in.at[0], qb, q=True)
    k_copies = scatter(1, k_in.at[0], kb)

    singles[4].wait()
    gates[0] = jnp.full((8, 128), gate_ref[0], jnp.float32)
    singles[5].wait()
    ids_copy = along_z(GAP, ids.at[0], ids.at[1], pass_send.at[4], pass_recv.at[4])
    gate_copy = along_z(GAP, gates.at[0], gates.at[1], pass_send.at[5], pass_recv.at[5])
    ids_copy.start()
    gate_copy.start()

    singles[3].wait()
    pointer = pointer_ref[0]
    column = 1 - pointer // N

    def keep_old(both, old, copy):
        copy.wait()

        def step(r, _):
            old[rows_of(r, 16), :] = both[column, rows_of(r, 16), :]
            return 0

        lax.fori_loop(0, BLK // 16, step, 0)

    keep_old(mk_both, mk_old, singles[0])
    keep_old(mv_both, mv_old, singles[1])
    for role, w in OWN:
        columns = rows_of(at_z(head_shift(role)), HD)
        mkb[role, w * BLK : (w + 1) * BLK] = mk_old[:, columns]
        mvb[role, w * BLK : (w + 1) * BLK] = mv_old[:, columns]

    for copy in own_q:
        copy.wait()
    for copy in q_copies:
        copy.wait_recv()
    near, far = slice(0, KEYS), slice(KEYS, SEG)
    relays = [
        along_z(GAP, qb.at[0, near], qb.at[1, near], pass_send.at[0], pass_recv.at[0]),
        along_z(-GAP, qb.at[1, far], qb.at[0, far], pass_send.at[1], pass_recv.at[1]),
    ]
    for copy in relays:
        copy.start()
    mk_copies = scatter(2, mk_old, mkb)
    v_copies = scatter(3, v_in.at[0], vb)
    mv_copies = scatter(4, mv_old, mvb)

    def block_at(role, u):
        return (z + u + (N - LEFT + head_shift(role))) & (N - 1)

    ids_copy.wait_recv()
    gate_copy.wait_recv()
    for role in ROLES:
        place = (ids[role] + pointer) & (2 * N - 1)
        for c in range(2 * KEYS // WIDE):
            w = lax.broadcasted_iota(jnp.int32, (N, WIDE), 1) // BLK + c * (WIDE // BLK)
            old = jnp.where(w >= HALF, N, 0)
            block = block_at(role, (w & (HALF - 1)) + HALF * role) + old
            picked = jnp.full((N, WIDE), LOW, jnp.float32)
            for t in range(N):
                picked = jnp.where(block == place[:, t : t + 1], 0.0, picked)
            bias[role, :, c * WIDE : (c + 1) * WIDE] = picked

    singles[2].wait()
    for copy in w_first:
        copy.wait_recv()
    mine = wb.at[pl.ds(y * xs, xs), core]
    w_second = [w_copy(xs - 1 + n, mine, mine, peer) for n, peer in enumerate(y_peers)]
    for copy in w_second:
        copy.start()

    def lane_max(m, s):
        for c in range(s.shape[1] // 128):
            m = jnp.maximum(m, s[:, c * 128 : (c + 1) * 128])
        return m

    def lane_sum(s):
        acc = s[:, :128]
        for c in range(1, s.shape[1] // 128):
            acc = acc + s[:, c * 128 : (c + 1) * 128]
        return acc

    chunks = range(KEYS // WIDE)

    def span(c):
        return slice(c * WIDE, (c + 1) * WIDE)

    def weigh(role, i, at, m, target, lane):
        highest = jnp.max(m, axis=1, keepdims=True)
        acc = jnp.zeros((PAIR, 128), jnp.float32)
        for c in chunks:
            p = jnp.exp2(scores[:, at + c * WIDE : at + (c + 1) * WIDE] - highest)
            target[role, rows_of(i, PAIR), span(c)] = p.astype(jnp.bfloat16)
            acc = acc + lane_sum(p)
        stats[role, rows_of(i, PAIR), lane : lane + 1] = highest
        stats[role, rows_of(i, PAIR), lane + 1 : lane + 2] = jnp.sum(acc, axis=1, keepdims=True)

    def picked_only(role, i, s, at):
        rows = [bias[role, pl.ds(block_at(role, 2 * i + b), 1), at] for b in (0, 1)]
        return jnp.concatenate([s[:BLK] + rows[0], s[BLK:] + rows[1]], axis=0)

    def segment_pair(role):
        def body(i, _):
            q = qb[role, rows_of(i, PAIR), :]
            row = lax.broadcasted_iota(jnp.int32, (PAIR, 128), 0)
            q_token = block_at(role, 2 * i + row // BLK) * BLK + (row & (BLK - 1))
            m_loc = m_seg = jnp.full((PAIR, 128), LOW, jnp.float32)
            for c in chunks:
                s = nt_dot(q, kb[role, span(c), :]) * SCALE
                kept = []
                for b in range(WIDE // BLK):
                    w = c * (WIDE // BLK) + b + HALF * role
                    lane = lax.broadcasted_iota(jnp.int32, (PAIR, 128), 1)
                    k_token = block_at(role, w) * BLK + lane
                    kept.append(
                        jnp.where(q_token >= k_token, s[:, b * BLK : (b + 1) * BLK], LOW)
                    )
                kept = jnp.concatenate(kept, axis=1)
                scores[:, span(c)] = kept
                m_loc = lane_max(m_loc, kept)
                s = picked_only(role, i, s, span(c))
                scores[:, KEYS + c * WIDE : KEYS + (c + 1) * WIDE] = s
                m_seg = lane_max(m_seg, s)
            weigh(role, i, 0, m_loc, p_loc, 0)
            weigh(role, i, KEYS, m_seg, p_seg, 2)
            return 0

        return body

    def old_pair(role):
        def body(i, _):
            q = qb[role, rows_of(i, PAIR), :]
            m_old = jnp.full((PAIR, 128), LOW, jnp.float32)
            for c in chunks:
                s = nt_dot(q, mkb[role, span(c), :]) * SCALE
                s = picked_only(role, i, s, slice(KEYS + c * WIDE, KEYS + (c + 1) * WIDE))
                scores[:, span(c)] = s
                m_old = lane_max(m_old, s)
            weigh(role, i, 0, m_old, p_old, 4)
            return 0

        return body

    for copy in own_k:
        copy.wait()
    for copy in k_copies:
        copy.wait_recv()
    quarter = HALF // 2
    lax.fori_loop(0, quarter, segment_pair(0), 0)
    lax.fori_loop(quarter, HALF, segment_pair(1), 0)
    relays[1].wait_recv()
    lax.fori_loop(quarter, HALF, segment_pair(0), 0)
    relays[0].wait_recv()
    lax.fori_loop(0, quarter, segment_pair(1), 0)

    for copy in w_second:
        copy.wait_recv()
    half = wb.at[:, core]
    w_third = w_copy(xs + ys - 2, half, half, sibling)
    w_third.start()

    for copy in mk_copies:
        copy.wait_recv()
    for role in ROLES:
        lax.fori_loop(0, HALF, old_pair(role), 0)

    for role in ROLES:
        for u in range(N):
            turned = jnp.transpose(stats[role, u * BLK : (u + 1) * BLK, :])
            for n in range(6):
                lines[role, n, u : u + 1, :] = turned[n : n + 1]
        loc, seg, old = (lines[role, n] + log2(lines[role, n + 1]) for n in (0, 2, 4))
        lse_out[role, 0] = loc
        lse_out[role, 1] = join(seg, old)
    lse_copies = [
        along_z(GAP, lse_out.at[0], lse_in.at[1], pass_send.at[2], pass_recv.at[2]),
        along_z(-GAP, lse_out.at[1], lse_in.at[0], pass_send.at[3], pass_recv.at[3]),
    ]
    for copy in lse_copies:
        copy.start()

    for copy in own_v:
        copy.wait()
    for copy in v_copies:
        copy.wait_recv()

    def value_pair(role):
        def body(i, _):
            rows = rows_of(i, PAIR)
            p = jnp.concatenate([p_loc[role, rows, :], p_seg[role, rows, :]], axis=0)
            acc = nn_dot(p, vb[role])
            parts[role, 0, rows, :] = acc[:PAIR]
            parts[role, 1, rows, :] = acc[PAIR:]
            return 0

        return body

    for role in ROLES:
        lax.fori_loop(0, HALF, value_pair(role), 0)

    for copy in mv_copies:
        copy.wait_recv()

    for copy in lse_copies:
        copy.wait_recv()
    factors = []
    for role in ROLES:
        gate = 1.0 / (1.0 + jnp.exp(-gates[role, :1, :1]))
        all_loc = join(lse_out[role, 0], lse_in[role, 0])
        all_mem = join(lse_out[role, 1], lse_in[role, 1])
        factors.append(
            [
                (1.0 - gate) * jnp.exp2(lines[role, 0] - all_loc),
                gate * jnp.exp2(lines[role, 2] - all_mem),
                gate * jnp.exp2(lines[role, 4] - all_mem),
            ]
        )

    def finish(role, u):
        rows = slice(u * BLK, (u + 1) * BLK)
        block = jnp.concatenate(
            [f[u : u + 1] for f in factors[role]] + [jnp.zeros((125, 128), jnp.float32)], axis=0
        )
        columns = jnp.transpose(block)
        got = nn_dot(p_old[role, rows, :], mvb[role])
        return (
            columns[:, 0:1] * parts[role, 0, rows, :]
            + columns[:, 1:2] * parts[role, 1, rows, :]
            + columns[:, 2:3] * got
        )

    order = [w for d in range(quarter) for w in (d, HALF - 1 - d)]
    part_copies = {}
    for w in order:
        for role in ROLES:
            part_out[role, w] = finish(role, w + HALF * (1 - role)).astype(jnp.bfloat16)
            copy = along_z(
                GAP if role == 0 else -GAP, part_out.at[role, w], part_in.at[1 - role, w],
                part_send.at[role, w], part_recv.at[1 - role, w],
            )
            copy.start()
            part_copies[role, w] = copy

    out_copies = {}
    for w in order:
        for role in ROLES:
            mine_f32 = finish(role, w + HALF * role)
            part_copies[1 - role, w].wait_recv()
            done = (mine_f32 + part_in[role, w].astype(jnp.float32)).astype(jnp.bfloat16)
            h = at_z(head_shift(role))
            o = -offset(role, w)
            if o == 0:
                heads[h] = done
            else:
                sent[role, w] = done
                copy = along_z(
                    o, sent.at[role, w], heads.at[h], out_send.at[role, w], out_recv.at[role, w]
                )
                copy.start()
                out_copies[role, w] = copy

    w_third.wait_recv()

    def weights(h):
        return wb[h].reshape(HD, wb.shape[-1])

    steps = [(role, w) for w in order for role in ROLES]
    for n, (role, w) in enumerate(steps):
        if (role, w) in out_copies:
            out_copies[role, w].wait_recv()
        h = at_z(LEFT - (w + HALF * role))
        term = nn_dot(heads[h], weights(h))
        if n == 0:
            total[...] = term
        elif n < len(steps) - 1:
            total[...] += term
        else:
            out_ref[0] = (total[...] + term).astype(jnp.bfloat16)

    for copy in w_first + w_second + [w_third]:
        copy.wait_send()
    for copy in q_copies + k_copies + mk_copies + v_copies + mv_copies + relays + lse_copies:
        copy.wait_send()
    for copy in [ids_copy, gate_copy, *part_copies.values(), *out_copies.values()]:
        copy.wait_send()


def local(
    dims,
    queries, seg_keys, seg_values, mem_keys, mem_values, block_ids, pointer, gate_bias, out_weight,
):
    width = queries.shape[2]
    ys, xs, cs = dims
    bf16, f32, i32 = jnp.bfloat16, jnp.float32, jnp.int32
    hbm = pl.BlockSpec(memory_space=pltpu.HBM)
    n_plane = xs + ys - 1
    dma = pltpu.SemaphoreType.DMA
    return pl.pallas_call(
        functools.partial(kernel, dims),
        out_shape=pltpu.VMEM(queries.shape, bf16),
        in_specs=[hbm] * 9,
        out_specs=pl.BlockSpec(memory_space=pltpu.VMEM),
        scratch_shapes=[
            pltpu.SMEM(pointer.shape, i32),
            pltpu.SMEM(gate_bias.shape, f32),
            pltpu.VMEM((2, N, N), i32),
            pltpu.VMEM((2, 8, 128), f32),
            pltpu.VMEM((2, SEG, HD), bf16),
            *[pltpu.VMEM((2, KEYS, HD), bf16) for _ in range(4)],
            pltpu.VMEM((2, BLK, width), bf16),
            pltpu.VMEM((2, BLK, width), bf16),
            pltpu.VMEM((BLK, width), bf16),
            pltpu.VMEM((BLK, width), bf16),
            pltpu.VMEM((2, N, 2 * KEYS), f32),
            pltpu.VMEM((PAIR, 2 * KEYS), f32),
            *[pltpu.VMEM((2, SEG, KEYS), bf16) for _ in range(3)],
            pltpu.VMEM((2, 2, SEG, HD), f32),
            pltpu.VMEM((2, SEG, 128), f32),
            pltpu.VMEM((2, 6, N, 128), f32),
            pltpu.VMEM((2, 2, N, 128), f32),
            pltpu.VMEM((2, 2, N, 128), f32),
            *[pltpu.VMEM((2, HALF, BLK, HD), bf16) for _ in range(3)],
            pltpu.VMEM((N, BLK, HD), bf16),
            pltpu.VMEM((ys * xs, cs, *out_weight.shape), bf16),
            pltpu.VMEM((BLK, width), f32),
            dma((5, 2, HALF)),
            dma((5, 2, HALF)),
            *[dma((2, HALF)) for _ in range(4)],
            dma((6,)),
            dma((6,)),
            dma((12,)),
            dma((n_plane,)),
            dma((n_plane,)),
        ],
        compiler_params=pltpu.CompilerParams(
            collective_id=0, has_side_effects=True, vmem_limit_bytes=60 * 1024 * 1024
        ),
        cost_estimate=pl.CostEstimate(
            flops=5_000_000_000, bytes_accessed=5_000_000, transcendentals=9_000_000
        ),
    )(pointer, gate_bias, block_ids, queries, seg_keys, seg_values, mem_keys, mem_values, out_weight)


def solution(mesh):
    dims = (4, 4, 2)
    in_specs = (
        P("dp", "mem", None),
        P("dp", "mem", None),
        P("dp", "mem", None),
        P("dp", None, "mem", None, None),
        P("dp", None, "mem", None, None),
        P("dp", None, "mem", None),
        P("dp"),
        P("mem"),
        P("dp", None),
    )
    return jax.shard_map(
        functools.partial(local, dims), mesh=mesh, in_specs=in_specs,
        out_specs=P("dp", "mem", None), check_vma=False,
    )
```

```python
import functools
import math

import jax
import jax.numpy as jnp
from jax import lax
from jax.experimental import pallas as pl
from jax.experimental.pallas import tpu as pltpu
from jax.sharding import PartitionSpec as P

HD = 128
BLK = 128
N = 16
HALF = N // 2
SEG = N * BLK
KEYS = HALF * BLK
PAIR = 2 * BLK
WIDE = 4 * BLK
LOW = -1e30
LOG2E = math.log2(math.e)
SCALE = LOG2E / math.sqrt(HD)
MESH = pl.DeviceIdType.MESH

GAP = 3
LEFT = 6
ROLES = (0, 1)


def offset(role, w):
    return LEFT - w if role == 0 else LEFT + GAP - HALF - w


def head_shift(role):
    return 0 if role == 0 else -GAP


FAR_FIRST = sorted(
    [(role, w) for role in ROLES for w in range(HALF) if offset(role, w)],
    key=lambda rw: -abs(offset(*rw)),
)
OWN = [(role, w) for role in ROLES for w in range(HALF) if offset(role, w) == 0]
PEERS = sorted({offset(*rw) for rw in FAR_FIRST} | {GAP, -GAP})


def nt_dot(a, b):
    return lax.dot_general(a, b, (((1,), (1,)), ((), ())), preferred_element_type=jnp.float32)


def nn_dot(a, b):
    return jnp.dot(a, b, preferred_element_type=jnp.float32)


def rows_of(index, size):
    return pl.ds(pl.multiple_of(index * size, size), size)


def log2(x):
    return jnp.log(x) * LOG2E


def join(a, b):
    m = jnp.maximum(a, b)
    return m + log2(jnp.exp2(a - m) + jnp.exp2(b - m))


def kernel(
    dims,
    pointer_in, gate_in, ids_in, q_in, k_in, v_in, mk_in, mv_in, w_in, out_ref,
    pointer_ref, gate_ref, ids, gates, qb, kb, vb, mkb, mvb, mk_both, mv_both, mk_old, mv_old,
    bias, scores, p_loc, p_seg, p_old, parts, stats, lines, lse_out, lse_in, part_out, part_in,
    sent, heads, wb, total,
    send_sem, recv_sem, out_send, out_recv, part_send, part_recv, pass_send, pass_recv,
    own_sem, w_send, w_recv,
):
    ys, xs, cs = dims
    z = lax.axis_index("mem")
    dp = lax.axis_index("dp")
    core = lax.rem(dp, cs)
    x = lax.rem(dp // cs, xs)
    y = dp // (cs * xs)

    def at_z(o):
        return lax.rem(z + (o + N), N)

    x_peers = [(y * xs + lax.rem(x + d, xs)) * cs + core for d in range(1, xs)]
    y_peers = [(lax.rem(y + d, ys) * xs + x) * cs + core for d in range(1, ys)]
    sibling = (y * xs + x) * cs + (1 - core)
    plane = x_peers + y_peers + [sibling]

    singles = [
        pltpu.make_async_copy(mk_in.at[0, :, 0], mk_both, own_sem.at[0]),
        pltpu.make_async_copy(mv_in.at[0, :, 0], mv_both, own_sem.at[1]),
        pltpu.make_async_copy(w_in, wb.at[y * xs + x, core], own_sem.at[2]),
        pltpu.make_async_copy(pointer_in, pointer_ref, own_sem.at[3]),
        pltpu.make_async_copy(gate_in, gate_ref, own_sem.at[4]),
        pltpu.make_async_copy(ids_in.at[0, :, 0], ids.at[0], own_sem.at[5]),
    ]

    def own_copies(n, src, dst, q):
        copies = []
        for role, w in OWN:
            row = w + (HALF * role if q else 0)
            copies.append(
                pltpu.make_async_copy(
                    src.at[0, :, rows_of(at_z(head_shift(role)), HD)],
                    dst.at[role, row * BLK : (row + 1) * BLK],
                    own_sem.at[n + role],
                )
            )
        return copies

    own_q, own_k = own_copies(6, q_in, qb, True), own_copies(8, k_in, kb, False)
    own_v = own_copies(10, v_in, vb, False)
    for copy in singles + own_q + own_k + own_v:
        copy.start()

    barrier = pltpu.get_barrier_semaphore()
    for o in PEERS:
        pl.semaphore_signal(barrier, inc=1, device_id={"mem": at_z(o)}, device_id_type=MESH)
    for peer in plane:
        pl.semaphore_signal(barrier, inc=1, device_id={"dp": peer}, device_id_type=MESH)
    pl.semaphore_wait(barrier, len(PEERS) + len(plane))

    def along_z(o, src, dst, sent_to, got):
        return pltpu.make_async_remote_copy(
            src_ref=src, dst_ref=dst, send_sem=sent_to, recv_sem=got,
            device_id={"mem": at_z(o)}, device_id_type=MESH,
        )

    def scatter(a, src, dst, q=False, held=0):
        copies = []
        for role, w in FAR_FIRST:
            o = offset(role, w)
            row = w + (HALF * role if q else 0)
            copy = along_z(
                o, src.at[:, rows_of(at_z(o + head_shift(role)), HD)],
                dst.at[role, row * BLK : (row + 1) * BLK],
                send_sem.at[a, role, w], recv_sem.at[a, role, w],
            )
            copies.append(copy)
        for copy in copies[: len(copies) - held]:
            copy.start()
        return copies

    def w_copy(n, src, dst, peer):
        return pltpu.make_async_remote_copy(
            src_ref=src, dst_ref=dst, send_sem=w_send.at[n], recv_sem=w_recv.at[n],
            device_id={"dp": peer}, device_id_type=MESH,
        )

    w_first = [
        w_copy(n, w_in, wb.at[y * xs + x, core], peer) for n, peer in enumerate(x_peers)
    ]
    for copy in w_first:
        copy.start()
    q_copies = scatter(0, q_in.at[0], qb, q=True)
    k_copies = scatter(1, k_in.at[0], kb)

    singles[4].wait()
    gates[0] = jnp.full((8, 128), gate_ref[0], jnp.float32)
    singles[5].wait()
    ids_copy = along_z(GAP, ids.at[0], ids.at[1], pass_send.at[4], pass_recv.at[4])
    gate_copy = along_z(GAP, gates.at[0], gates.at[1], pass_send.at[5], pass_recv.at[5])
    ids_copy.start()
    gate_copy.start()

    singles[3].wait()
    pointer = pointer_ref[0]
    column = 1 - pointer // N

    def keep_old(both, old, copy):
        copy.wait()

        def step(r, _):
            old[rows_of(r, 16), :] = both[column, rows_of(r, 16), :]
            return 0

        lax.fori_loop(0, BLK // 16, step, 0)

    keep_old(mk_both, mk_old, singles[0])
    keep_old(mv_both, mv_old, singles[1])
    for role, w in OWN:
        columns = rows_of(at_z(head_shift(role)), HD)
        mkb[role, w * BLK : (w + 1) * BLK] = mk_old[:, columns]
        mvb[role, w * BLK : (w + 1) * BLK] = mv_old[:, columns]

    near, far = slice(0, KEYS), slice(KEYS, SEG)
    relays = [
        along_z(GAP, qb.at[0, near], qb.at[1, near], pass_send.at[0], pass_recv.at[0]),
        along_z(-GAP, qb.at[1, far], qb.at[0, far], pass_send.at[1], pass_recv.at[1]),
    ]
    for relay, own_copy, role in zip(relays, own_q, ROLES, strict=True):
        own_copy.wait()
        for copy, (copy_role, _) in zip(q_copies, FAR_FIRST, strict=True):
            if copy_role == role:
                copy.wait_recv()
        relay.start()
    mk_copies = scatter(2, mk_old, mkb)
    v_copies = scatter(3, v_in.at[0], vb)
    mv_copies = scatter(4, mv_old, mvb, held=4)

    def block_at(role, u):
        return (z + u + (N - LEFT + head_shift(role))) & (N - 1)

    ids_copy.wait_recv()
    gate_copy.wait_recv()
    for role in ROLES:
        place = (ids[role] + pointer) & (2 * N - 1)
        for c in range(2 * KEYS // WIDE):
            w = lax.broadcasted_iota(jnp.int32, (N, WIDE), 1) // BLK + c * (WIDE // BLK)
            old = jnp.where(w >= HALF, N, 0)
            block = block_at(role, (w & (HALF - 1)) + HALF * role) + old
            picked = jnp.full((N, WIDE), LOW, jnp.float32)
            for t in range(N):
                picked = jnp.where(block == place[:, t : t + 1], 0.0, picked)
            bias[role, :, c * WIDE : (c + 1) * WIDE] = picked

    singles[2].wait()
    for copy in w_first:
        copy.wait_recv()
    mine = wb.at[pl.ds(y * xs, xs), core]
    w_second = [w_copy(xs - 1 + n, mine, mine, peer) for n, peer in enumerate(y_peers)]
    for copy in w_second:
        copy.start()

    def lane_max(m, s):
        for c in range(s.shape[1] // 128):
            m = jnp.maximum(m, s[:, c * 128 : (c + 1) * 128])
        return m

    def lane_sum(s):
        acc = s[:, :128]
        for c in range(1, s.shape[1] // 128):
            acc = acc + s[:, c * 128 : (c + 1) * 128]
        return acc

    chunks = range(KEYS // WIDE)

    def span(c):
        return slice(c * WIDE, (c + 1) * WIDE)

    def weigh(role, i, at, m, target, lane):
        highest = jnp.max(m, axis=1, keepdims=True)
        acc = jnp.zeros((PAIR, 128), jnp.float32)
        for c in chunks:
            p = jnp.exp2(scores[:, at + c * WIDE : at + (c + 1) * WIDE] - highest)
            target[role, rows_of(i, PAIR), span(c)] = p.astype(jnp.bfloat16)
            acc = acc + lane_sum(p)
        stats[role, rows_of(i, PAIR), lane : lane + 1] = highest
        stats[role, rows_of(i, PAIR), lane + 1 : lane + 2] = jnp.sum(acc, axis=1, keepdims=True)

    def picked_only(role, i, s, at):
        rows = [bias[role, pl.ds(block_at(role, 2 * i + b), 1), at] for b in (0, 1)]
        return jnp.concatenate([s[:BLK] + rows[0], s[BLK:] + rows[1]], axis=0)

    def segment_pair(role):
        def body(i, _):
            q = qb[role, rows_of(i, PAIR), :]
            row = lax.broadcasted_iota(jnp.int32, (PAIR, 128), 0)
            q_token = block_at(role, 2 * i + row // BLK) * BLK + (row & (BLK - 1))
            m_loc = m_seg = jnp.full((PAIR, 128), LOW, jnp.float32)
            for c in chunks:
                s = nt_dot(q, kb[role, span(c), :]) * SCALE
                kept = []
                for b in range(WIDE // BLK):
                    w = c * (WIDE // BLK) + b + HALF * role
                    lane = lax.broadcasted_iota(jnp.int32, (PAIR, 128), 1)
                    k_token = block_at(role, w) * BLK + lane
                    kept.append(
                        jnp.where(q_token >= k_token, s[:, b * BLK : (b + 1) * BLK], LOW)
                    )
                kept = jnp.concatenate(kept, axis=1)
                scores[:, span(c)] = kept
                m_loc = lane_max(m_loc, kept)
                s = picked_only(role, i, s, span(c))
                scores[:, KEYS + c * WIDE : KEYS + (c + 1) * WIDE] = s
                m_seg = lane_max(m_seg, s)
            weigh(role, i, 0, m_loc, p_loc, 0)
            weigh(role, i, KEYS, m_seg, p_seg, 2)
            return 0

        return body

    def old_pair(role):
        def body(i, _):
            q = qb[role, rows_of(i, PAIR), :]
            m_old = jnp.full((PAIR, 128), LOW, jnp.float32)
            for c in chunks:
                s = nt_dot(q, mkb[role, span(c), :]) * SCALE
                s = picked_only(role, i, s, slice(KEYS + c * WIDE, KEYS + (c + 1) * WIDE))
                scores[:, span(c)] = s
                m_old = lane_max(m_old, s)
            weigh(role, i, 0, m_old, p_old, 4)
            return 0

        return body

    for copy in own_k:
        copy.wait()
    for copy in k_copies:
        copy.wait_recv()
    quarter = HALF // 2
    lax.fori_loop(0, quarter, segment_pair(0), 0)
    lax.fori_loop(quarter, HALF, segment_pair(1), 0)
    relays[1].wait_recv()
    lax.fori_loop(quarter, HALF, segment_pair(0), 0)
    relays[0].wait_recv()
    lax.fori_loop(0, quarter, segment_pair(1), 0)

    for copy in w_second:
        copy.wait_recv()
    half = wb.at[:, core]
    w_third = w_copy(xs + ys - 2, half, half, sibling)
    w_third.start()

    for copy in mk_copies:
        copy.wait_recv()
    lse_copies = [
        along_z(GAP, lse_out.at[0], lse_in.at[1], pass_send.at[2], pass_recv.at[2]),
        along_z(-GAP, lse_out.at[1], lse_in.at[0], pass_send.at[3], pass_recv.at[3]),
    ]
    for role in ROLES:
        lax.fori_loop(0, HALF, old_pair(role), 0)
        for u in range(N):
            turned = jnp.transpose(stats[role, u * BLK : (u + 1) * BLK, :])
            for n in range(6):
                lines[role, n, u : u + 1, :] = turned[n : n + 1]
        loc, seg, old = (lines[role, n] + log2(lines[role, n + 1]) for n in (0, 2, 4))
        lse_out[role, 0] = loc
        lse_out[role, 1] = join(seg, old)
        lse_copies[role].start()
    for copy in mv_copies[-4:]:
        copy.start()

    for copy in own_v:
        copy.wait()
    for copy in v_copies:
        copy.wait_recv()

    def value_pair(role):
        def body(i, _):
            rows = rows_of(i, PAIR)
            p = jnp.concatenate([p_loc[role, rows, :], p_seg[role, rows, :]], axis=0)
            acc = nn_dot(p, vb[role])
            parts[role, 0, rows, :] = acc[:PAIR]
            parts[role, 1, rows, :] = acc[PAIR:]
            return 0

        return body

    for role in ROLES:
        lax.fori_loop(0, HALF, value_pair(role), 0)

    for copy in mv_copies:
        copy.wait_recv()

    for copy in lse_copies:
        copy.wait_recv()
    factors = []
    for role in ROLES:
        gate = 1.0 / (1.0 + jnp.exp(-gates[role, :1, :1]))
        all_loc = join(lse_out[role, 0], lse_in[role, 0])
        all_mem = join(lse_out[role, 1], lse_in[role, 1])
        factors.append(
            [
                (1.0 - gate) * jnp.exp2(lines[role, 0] - all_loc),
                gate * jnp.exp2(lines[role, 2] - all_mem),
                gate * jnp.exp2(lines[role, 4] - all_mem),
            ]
        )

    def finish(role, u):
        rows = slice(u * BLK, (u + 1) * BLK)
        block = jnp.concatenate(
            [f[u : u + 1] for f in factors[role]] + [jnp.zeros((125, 128), jnp.float32)], axis=0
        )
        columns = jnp.transpose(block)
        got = nn_dot(p_old[role, rows, :], mvb[role])
        return (
            columns[:, 0:1] * parts[role, 0, rows, :]
            + columns[:, 1:2] * parts[role, 1, rows, :]
            + columns[:, 2:3] * got
        )

    order = [w for d in range(quarter) for w in (d, HALF - 1 - d)]
    part_copies = {}
    for w in order:
        for role in ROLES:
            part_out[role, w] = finish(role, w + HALF * (1 - role)).astype(jnp.bfloat16)
            copy = along_z(
                GAP if role == 0 else -GAP, part_out.at[role, w], part_in.at[1 - role, w],
                part_send.at[role, w], part_recv.at[1 - role, w],
            )
            copy.start()
            part_copies[role, w] = copy

    out_copies = {}
    for w in order:
        for role in ROLES:
            mine_f32 = finish(role, w + HALF * role)
            part_copies[1 - role, w].wait_recv()
            done = (mine_f32 + part_in[role, w].astype(jnp.float32)).astype(jnp.bfloat16)
            h = at_z(head_shift(role))
            o = -offset(role, w)
            if o == 0:
                heads[h] = done
            else:
                sent[role, w] = done
                copy = along_z(
                    o, sent.at[role, w], heads.at[h], out_send.at[role, w], out_recv.at[role, w]
                )
                copy.start()
                out_copies[role, w] = copy

    w_third.wait_recv()

    def weights(h):
        return wb[h].reshape(HD, wb.shape[-1])

    steps = [(role, w) for w in order for role in ROLES]
    for n, (role, w) in enumerate(steps):
        if (role, w) in out_copies:
            out_copies[role, w].wait_recv()
        h = at_z(LEFT - (w + HALF * role))
        term = nn_dot(heads[h], weights(h))
        if n == 0:
            total[...] = term
        elif n < len(steps) - 1:
            total[...] += term
        else:
            out_ref[0] = (total[...] + term).astype(jnp.bfloat16)

    for copy in w_first + w_second + [w_third]:
        copy.wait_send()
    for copy in q_copies + k_copies + mk_copies + v_copies + mv_copies + relays + lse_copies:
        copy.wait_send()
    for copy in [ids_copy, gate_copy, *part_copies.values(), *out_copies.values()]:
        copy.wait_send()


def local(
    dims,
    queries, seg_keys, seg_values, mem_keys, mem_values, block_ids, pointer, gate_bias, out_weight,
):
    width = queries.shape[2]
    ys, xs, cs = dims
    bf16, f32, i32 = jnp.bfloat16, jnp.float32, jnp.int32
    hbm = pl.BlockSpec(memory_space=pltpu.HBM)
    n_plane = xs + ys - 1
    dma = pltpu.SemaphoreType.DMA
    return pl.pallas_call(
        functools.partial(kernel, dims),
        out_shape=pltpu.VMEM(queries.shape, bf16),
        in_specs=[hbm] * 9,
        out_specs=pl.BlockSpec(memory_space=pltpu.VMEM),
        scratch_shapes=[
            pltpu.SMEM(pointer.shape, i32),
            pltpu.SMEM(gate_bias.shape, f32),
            pltpu.VMEM((2, N, N), i32),
            pltpu.VMEM((2, 8, 128), f32),
            pltpu.VMEM((2, SEG, HD), bf16),
            *[pltpu.VMEM((2, KEYS, HD), bf16) for _ in range(4)],
            pltpu.VMEM((2, BLK, width), bf16),
            pltpu.VMEM((2, BLK, width), bf16),
            pltpu.VMEM((BLK, width), bf16),
            pltpu.VMEM((BLK, width), bf16),
            pltpu.VMEM((2, N, 2 * KEYS), f32),
            pltpu.VMEM((PAIR, 2 * KEYS), f32),
            *[pltpu.VMEM((2, SEG, KEYS), bf16) for _ in range(3)],
            pltpu.VMEM((2, 2, SEG, HD), f32),
            pltpu.VMEM((2, SEG, 128), f32),
            pltpu.VMEM((2, 6, N, 128), f32),
            pltpu.VMEM((2, 2, N, 128), f32),
            pltpu.VMEM((2, 2, N, 128), f32),
            *[pltpu.VMEM((2, HALF, BLK, HD), bf16) for _ in range(3)],
            pltpu.VMEM((N, BLK, HD), bf16),
            pltpu.VMEM((ys * xs, cs, *out_weight.shape), bf16),
            pltpu.VMEM((BLK, width), f32),
            dma((5, 2, HALF)),
            dma((5, 2, HALF)),
            *[dma((2, HALF)) for _ in range(4)],
            dma((6,)),
            dma((6,)),
            dma((12,)),
            dma((n_plane,)),
            dma((n_plane,)),
        ],
        compiler_params=pltpu.CompilerParams(
            collective_id=0, has_side_effects=True, vmem_limit_bytes=60 * 1024 * 1024
        ),
        cost_estimate=pl.CostEstimate(
            flops=5_000_000_000, bytes_accessed=5_000_000, transcendentals=9_000_000
        ),
    )(pointer, gate_bias, block_ids, queries, seg_keys, seg_values, mem_keys, mem_values, out_weight)


def solution(mesh):
    dims = (4, 4, 2)
    in_specs = (
        P("dp", "mem", None),
        P("dp", "mem", None),
        P("dp", "mem", None),
        P("dp", None, "mem", None, None),
        P("dp", None, "mem", None, None),
        P("dp", None, "mem", None),
        P("dp"),
        P("mem"),
        P("dp", None),
    )
    return jax.shard_map(
        functools.partial(local, dims), mesh=mesh, in_specs=in_specs,
        out_specs=P("dp", "mem", None), check_vma=False,
    )
```
